128 devices in a mesh: site: 4 (over x), bond: 32 (over z, y, core).
Axes of the slice: x: 4, y: 4, z: 4, core: 2. Of those that a mesh axis runs over, the one named last changes fastest.
Arguments:
- start_rows: bfloat16 [1024, 4096], P(None, 'bond'), may hold values from -6 to 6
- site_tensors: bfloat16 [4, 4096, 8, 4096], P('site', None, None, 'bond'), may hold values from -0.09375 to 0.09375
- block_scales: float32 [4, 8, 32], P('site', None, 'bond'), may hold values from 0.25 to 1
- displacement: float32 [4, 8, 8], P('site'), may hold values from -0.9 to 0.9
- outcomes: int32 [4, 1024], P('site'), may hold values from 0 to 7
Outputs:
- leaving: bfloat16 [4, 1024, 4096], P('site', None, 'bond')
- log_norms: float32 [4, 1024], P('site')
The draws below stay inside these ranges and needn't reach their ends.
Inputs may be any that keep to these rules, and one draw needn't show every extreme that they name: outcomes index the second dimension of displacement.
All inputs are finite; a program needn't handle non-finite values.
Results may differ from the reference program's by a relative error of at most 0.014.
Values may be sent and summed in bfloat16 or wider, within the bound.
No kernel may reach another device: no remote copies, remote signals or barrier semaphores. Data moves between devices by JAX's collectives and lax.ppermute only.
A program may use at most 64 MiB of HBM per device.

```python
import math
import jax
import jax.numpy as jnp
from jax import lax

CHI = 4096
PHYS = 8
BLOCK = 128
SITES = 4
ALLROWS = 1024


def touch_ends(values, own_key, low, high):
    longest = values.shape.index(max(values.shape))
    spots = []
    for shift in (0, 1):
        where = [jax.random.randint(jax.random.fold_in(own_key, axis), (), 0, length) for axis, length in enumerate(values.shape)]
        where[longest] = (where[longest] + shift) % values.shape[longest]
        spots.append(tuple(where))
    return values.at[spots[0]].set(low).at[spots[1]].set(high)


def block_scale(own_key, dims, shards, least, high):
    def one(axis_at, blocks):
        steps = jax.random.uniform(jax.random.fold_in(jax.random.fold_in(own_key, 6), axis_at), (blocks,), jnp.float32, least / len(shards), high / len(shards))
        return jnp.repeat(jnp.exp(steps), dims[axis_at] // blocks).reshape((-1,) + (1,) * (len(dims) - axis_at - 1))

    loudness = one(*shards[0])
    for cut in shards[1:]:
        loudness = loudness * one(*cut)
    return loudness


def gaussian(stream_key, dims, width, most, split=(), held_as=jnp.bfloat16):
    factor_of = block_scale(stream_key, dims, split, -0.22, 0.18) if split else 1.0
    drawn = jax.random.normal(stream_key, dims, jnp.float32) * width * factor_of
    return jnp.minimum(jnp.maximum(drawn, -most), most).astype(held_as)


def setup_inputs(seed: int = 0) -> dict:
    key_of = jax.random.split(jax.random.key(seed), 6)
    return {
        "start_rows": gaussian(key_of[0], (ALLROWS, CHI), 1.0, 6.0, ((1, 32),)),
        "site_tensors": gaussian(key_of[1], (SITES, CHI, PHYS, CHI), CHI ** -0.5, 0.09375, ((0, 4), (3, 32))),
        "block_scales": jnp.clip(jnp.exp(math.log(1.0) - 1.3862944 * jax.random.uniform(key_of[2], (SITES, PHYS, CHI // BLOCK), jnp.float32) ** block_scale(key_of[2], (SITES, PHYS, CHI // BLOCK), ((0, 4), (2, 32)), -0.2, 0.2)), 0.25, 1.0),
        "displacement": gaussian(key_of[3], (SITES, PHYS, PHYS), 0.3, 0.9, ((0, 4),), jnp.float32),
        "outcomes": touch_ends(jax.random.randint(key_of[4], (SITES, ALLROWS), 0, PHYS), jax.random.fold_in(key_of[4], 1), 0, PHYS - 1).astype(jnp.int32),
    }


def reference(start_rows, site_tensors, block_scales, displacement, outcomes):
    entering = start_rows
    leaves = []
    logs = []
    for k in range(SITES):
        xf = entering.astype(jnp.float32)
        norm = jnp.sqrt(lax.optimization_barrier(jnp.mean(xf * xf, axis=1)) + 1e-06)
        logs.append(jnp.log(norm))
        prod = jnp.dot(entering, site_tensors[k].reshape(CHI, PHYS * CHI), preferred_element_type=jnp.float32)
        prod = prod.reshape(ALLROWS, PHYS, CHI // BLOCK, BLOCK) * block_scales[k][None, :, :, None]
        prod = prod.reshape(ALLROWS, PHYS, CHI)
        weight = displacement[k][outcomes[k]]
        mixed = jnp.einsum('bp,bpr->br', weight, prod)
        leave = (mixed / norm[:, None]).astype(jnp.bfloat16)
        leaves.append(leave)
        entering = leave
    return (jnp.stack(leaves), jnp.stack(logs))
```

```python
import functools

import jax
import jax.numpy as jnp
from jax import lax
from jax.experimental import pallas as pl
from jax.experimental.pallas import tpu as pltpu
from jax.sharding import Mesh, PartitionSpec as P

ROWS = 256
NZ, NY, NC = 4, 4, 2
BOND = ("z", "y", "core")


def contract_kernel(y_ref, x_ref, w_ref, own_ref, part_ref, mixed_ref, other_ref):
    phys = w_ref.shape[0]
    y = y_ref[0]
    blocks = []
    for z in range(NZ):
        for yy in range(NY):
            blocks.append(x_ref[z, lax.rem(y - yy + NY, NY)])
    rows = jnp.concatenate(blocks, axis=1)
    cols = mixed_ref.shape[1]
    squares = None
    for block in blocks:
        wide = block.astype(jnp.float32)
        squares = wide * wide if squares is None else squares + wide * wide
    mixed = jnp.zeros(mixed_ref.shape, jnp.float32)
    other = jnp.zeros(mixed_ref.shape, jnp.float32)
    for p in range(phys):
        prod = jnp.dot(rows, w_ref[p], preferred_element_type=jnp.float32)
        mixed += own_ref[:, p : p + 1] * prod[:, :cols]
        other += part_ref[:, p : p + 1] * prod[:, cols:]
    total = jnp.broadcast_to(jnp.sum(squares, axis=1, keepdims=True), mixed_ref.shape)
    mixed_ref[...] = mixed
    other_ref[:, :cols] = other
    other_ref[:, cols:] = total


def contract(y, x, w, own, part):
    rows, cols = x.shape[2], x.shape[3]
    vmem = pl.BlockSpec(memory_space=pltpu.VMEM)
    return pl.pallas_call(
        contract_kernel,
        out_shape=(
            jax.ShapeDtypeStruct((rows, cols), jnp.float32),
            jax.ShapeDtypeStruct((rows, 2 * cols), jnp.float32),
        ),
        in_specs=[pl.BlockSpec(memory_space=pltpu.SMEM)] + [vmem] * 4,
        out_specs=(vmem, vmem),
        compiler_params=pltpu.CompilerParams(vmem_limit_bytes=24 * 2**20),
    )(y, x, w, own, part)


def local(start_rows, site_tensors, block_scales, displacement, outcomes):
    sites = lax.axis_size("site")
    chi, phys, cols = site_tensors.shape[1:]
    allrows = start_rows.shape[0]
    ngroups = allrows // ROWS
    ticks = ngroups + sites - 1
    position = lax.axis_index("site")
    core = lax.axis_index("core")
    y = lax.axis_index("y")
    swap = [(0, 1), (1, 0)]

    def to_partner(value):
        return lax.ppermute(value, "core", swap)

    def diagonals(value):
        return jnp.stack([
            lax.ppermute(
                value,
                ("site", "y"),
                [
                    (s * NY + q, ((s + 1) % sites) * NY + (q + shift) % NY)
                    for s in range(sites)
                    for q in range(NY)
                ],
            )
            for shift in range(NY)
        ])

    def along_z(value):
        return lax.all_to_all(jnp.broadcast_to(value[None], (NZ,) + value.shape), "z", 0, 0)

    def start_piece(batch):
        return start_rows[batch * ROWS : (batch + 1) * ROWS]

    tensor = site_tensors[0].reshape(chi // (NC * cols), NC, cols, phys, cols)
    keep = lax.dynamic_index_in_dim(tensor, core, 1, keepdims=False)
    give = lax.dynamic_index_in_dim(tensor, 1 - core, 1, keepdims=False)
    got = to_partner(give)
    half = chi // NC
    w = jnp.concatenate(
        [jnp.swapaxes(part.reshape(half, phys, cols), 0, 1) for part in (keep, got)], axis=2
    )
    scale = block_scales[0][:, 0]
    partner_scale = to_partner(scale)
    onehot = (outcomes[0][:, None] == jnp.arange(phys, dtype=jnp.int32)[None, :]).astype(jnp.float32)
    weight = jnp.dot(onehot, displacement[0], precision=lax.Precision.HIGHEST)
    own_coef = weight * scale[None, :]
    part_coef = weight * partner_scale[None, :]
    y_arr = y[None].astype(jnp.int32)

    gathered = along_z(diagonals(start_piece(0)))
    leaves, logs = [], []
    for step in range(ticks):
        batch = jnp.clip(step - position, 0, ngroups - 1)
        first = batch * ROWS
        own = lax.dynamic_slice_in_dim(own_coef, first, ROWS, 0)
        part = lax.dynamic_slice_in_dim(part_coef, first, ROWS, 0)
        mixed, other = contract(y_arr, gathered, w, own, part)
        arrived = to_partner(other)
        norm = jnp.sqrt((other[:, cols:] + arrived[:, cols:]) / chi + 1e-06)
        leave = ((mixed + arrived[:, :cols]) / norm).astype(jnp.bfloat16)
        leaves.append(leave)
        logs.append(jnp.log(norm[:, 0]))
        if step + 1 < ticks:
            ahead = start_piece(min(step + 1, ngroups - 1))
            gathered = along_z(diagonals(jnp.where(position == sites - 1, ahead, leave)))
    out_leave = lax.dynamic_slice_in_dim(jnp.concatenate(leaves, 0), position * ROWS, allrows, 0)
    out_logs = lax.dynamic_slice_in_dim(jnp.concatenate(logs, 0), position * ROWS, allrows, 0)
    return (out_leave[None], out_logs[None])


def solution(mesh):
    fine = Mesh(mesh.devices.reshape(-1, NZ, NY, NC), ("site",) + BOND)
    return jax.shard_map(
        local,
        mesh=fine,
        in_specs=(
            P(None, BOND),
            P("site", None, None, BOND),
            P("site", None, BOND),
            P("site", None, None),
            P("site", None),
        ),
        out_specs=(P("site", None, BOND), P("site", None)),
        check_vma=False,
    )
```

```python
import jax
import jax.numpy as jnp
from jax import lax
from jax.experimental import pallas as pl
from jax.experimental.pallas import tpu as pltpu
from jax.sharding import Mesh, PartitionSpec as P

ROWS = 256
NZ, NY, NC = 4, 4, 2
PLANE = ("z", "y")
BOND = ("z", "y", "core")
VMEM = pl.BlockSpec(memory_space=pltpu.VMEM)
SMEM = pl.BlockSpec(memory_space=pltpu.SMEM)
HBM = pl.BlockSpec(memory_space=pltpu.HBM)


def give_kernel(parity_ref, t_ref, out_ref, held, sems):
    blocks, size = held.shape[:2]
    parity = parity_ref[0]
    copies = [pltpu.make_async_copy(t_ref.at[j, parity], held.at[j], sems.at[j]) for j in range(blocks)]
    for copy in copies:
        copy.start()
    for j in range(blocks):
        copies[j].wait()
        out_ref[:, j * size : (j + 1) * size, :] = jnp.swapaxes(held[j], 0, 1)


def join_kernel(parity_ref, t_ref, got_ref, out_ref, held, sems, got_sem):
    blocks, size = held.shape[:2]
    cols = held.shape[3]
    parity = parity_ref[0]
    copies = [pltpu.make_async_copy(t_ref.at[j, parity], held.at[j], sems.at[j]) for j in range(blocks)]
    for copy in copies:
        copy.start()
    right = pltpu.make_async_copy(got_ref, out_ref.at[:, :, cols:], got_sem)
    right.start()
    for j in range(blocks):
        copies[j].wait()
        out_ref[:, j * size : (j + 1) * size, :cols] = jnp.swapaxes(held[j], 0, 1)
    right.wait()


def give(parity, t):
    blocks, _, size, phys, cols = t.shape
    return pl.pallas_call(
        give_kernel,
        out_shape=jax.ShapeDtypeStruct((phys, blocks * size, cols), t.dtype),
        in_specs=[SMEM, HBM],
        out_specs=VMEM,
        scratch_shapes=[
            pltpu.VMEM((blocks, size, phys, cols), t.dtype),
            pltpu.SemaphoreType.DMA((blocks,)),
        ],
        compiler_params=pltpu.CompilerParams(vmem_limit_bytes=56 * 2**20),
    )(parity, t)


def join(parity, t, got):
    blocks, _, size, phys, cols = t.shape
    return pl.pallas_call(
        join_kernel,
        out_shape=pltpu.VMEM((phys, blocks * size, 2 * cols), t.dtype),
        in_specs=[SMEM, HBM, HBM],
        out_specs=VMEM,
        scratch_shapes=[
            pltpu.VMEM((blocks, size, phys, cols), t.dtype),
            pltpu.SemaphoreType.DMA((blocks,)),
            pltpu.SemaphoreType.DMA,
        ],
        compiler_params=pltpu.CompilerParams(vmem_limit_bytes=48 * 2**20),
    )(parity, t, got)


def contract_kernel(x_ref, w_ref, own_ref, part_ref, mixed_ref, other_ref):
    blocks = [x_ref[j] for j in range(x_ref.shape[0])]
    rows = jnp.concatenate(blocks, axis=1)
    cols = mixed_ref.shape[1]
    squares = None
    for block in blocks:
        wide = block.astype(jnp.float32)
        squares = wide * wide if squares is None else squares + wide * wide
    mixed = jnp.zeros(mixed_ref.shape, jnp.float32)
    other = jnp.zeros(mixed_ref.shape, jnp.float32)
    for p in range(w_ref.shape[0]):
        prod = jnp.dot(rows, w_ref[p], preferred_element_type=jnp.float32)
        mixed += own_ref[:, p : p + 1] * prod[:, :cols]
        other += part_ref[:, p : p + 1] * prod[:, cols:]
    total = jnp.broadcast_to(jnp.sum(squares, axis=1, keepdims=True), mixed_ref.shape)
    mixed_ref[...] = mixed
    other_ref[:, :cols] = other
    other_ref[:, cols:] = total


def contract(x, w, own, part):
    rows, cols = x.shape[1:]
    return pl.pallas_call(
        contract_kernel,
        out_shape=(
            jax.ShapeDtypeStruct((rows, cols), jnp.float32),
            jax.ShapeDtypeStruct((rows, 2 * cols), jnp.float32),
        ),
        in_specs=[VMEM] * 4,
        out_specs=(VMEM, VMEM),
        compiler_params=pltpu.CompilerParams(vmem_limit_bytes=16 * 2**20),
    )(x, w, own, part)


def local(start_rows, site_tensors, block_scales, displacement, outcomes):
    sites = lax.axis_size("site")
    chi, phys, cols = site_tensors.shape[1:]
    allrows = start_rows.shape[0]
    ngroups = allrows // ROWS
    bodies = ngroups + sites - 1
    position = lax.axis_index("site")
    core = lax.axis_index("core")[None].astype(jnp.int32)

    def to_partner(value):
        return lax.ppermute(value, "core", [(0, 1), (1, 0)])

    def ahead(value):
        return lax.ppermute(value, "site", [(s, (s + 1) % sites) for s in range(sites)])

    def plane_gather(value):
        copies = jnp.broadcast_to(value[None], (NZ * NY,) + value.shape)
        return lax.all_to_all(copies, PLANE, 0, 0)

    def start_piece(batch):
        first = min(batch, ngroups - 1) * ROWS
        return start_rows[first : first + ROWS]

    tensor = site_tensors[0].reshape(NZ * NY, NC, cols, phys, cols)
    scale = block_scales[0][:, 0]
    partner_scale = to_partner(scale)
    onehot = (outcomes[0][:, None] == jnp.arange(phys, dtype=jnp.int32)[None, :]).astype(jnp.float32)
    weight = jnp.dot(onehot, displacement[0], precision=lax.Precision.HIGHEST)
    own_coef = weight * scale[None, :]
    part_coef = weight * partner_scale[None, :]
    def coefficients(body):
        first = jnp.clip(body - position, 0, ngroups - 1) * ROWS
        return [lax.dynamic_slice_in_dim(c, first, ROWS, 0) for c in (own_coef, part_coef)]

    coefs = [coefficients(body) for body in range(bodies)]
    sent = give(1 - core, tensor)
    piece, sent, coefs, closing = lax.optimization_barrier(
        (start_piece(0), sent, coefs, position == sites - 1)
    )
    got = to_partner(sent)
    gathered = plane_gather(piece)
    gathered, got = lax.optimization_barrier((gathered, got))
    w = join(core, tensor, got)

    leaves, norms = [], []
    for body in range(bodies):
        mixed, other = contract(gathered, w, *coefs[body])
        arrived = to_partner(other)
        norm = jnp.sqrt((other[:, cols:] + arrived[:, cols:]) / chi + 1e-06)
        leave = ((mixed + arrived[:, :cols]) / norm).astype(jnp.bfloat16)
        if body + 1 < bodies:
            onward = ahead(jnp.where(closing, start_piece(body + 1), leave))
        leaves.append(leave)
        norms.append(norm[:, 0])
        if body + 1 < bodies:
            onward, leaves[-1], norms[-1] = lax.optimization_barrier((onward, leaves[-1], norms[-1]))
            gathered = plane_gather(onward)
    offset = position * ROWS
    out_leave = lax.dynamic_slice_in_dim(jnp.concatenate(leaves, 0), offset, allrows, 0)
    out_norm = lax.dynamic_slice_in_dim(jnp.concatenate(norms, 0), offset, allrows, 0)
    return (out_leave[None], jnp.log(out_norm)[None])


def solution(mesh):
    fine = Mesh(mesh.devices.reshape(-1, NZ, NY, NC), ("site",) + BOND)
    return jax.shard_map(
        local,
        mesh=fine,
        in_specs=(
            P(None, BOND),
            P("site", None, None, BOND),
            P("site", None, BOND),
            P("site", None, None),
            P("site", None),
        ),
        out_specs=(P("site", None, BOND), P("site", None)),
        check_vma=False,
    )
```

```python
import itertools

import jax
import jax.numpy as jnp
from jax import lax
from jax.experimental import pallas as pl
from jax.experimental.pallas import tpu as pltpu
from jax.sharding import Mesh, PartitionSpec as P

ROWS = 256
STRIDE = 256
NZ, NY, NC = 4, 4, 2
FIRST = (0, 1, 2, 3)
SECOND = (2, 1, 3)
BOND = ("z", "y", "core")
VMEM = pl.BlockSpec(memory_space=pltpu.VMEM)
HBM = pl.BlockSpec(memory_space=pltpu.HBM)


def fetches(parity, t_ref, held, sems):
    z, y = lax.axis_index("z"), lax.axis_index("y")
    copies = []
    for i, second in enumerate((0,) + SECOND):
        for k, first in enumerate(FIRST):
            back_z = (1 - parity) * second + parity * first
            back_y = (1 - parity) * first + parity * second
            block = lax.rem(z - back_z + NZ, NZ) * NY + lax.rem(y - back_y + NY, NY)
            j = i * NY + k
            copies.append(pltpu.make_async_copy(t_ref.at[block, parity], held.at[j], sems.at[j]))
    return copies


def give_kernel(t_ref, out_ref, held, sems):
    blocks, size = held.shape[:2]
    copies = fetches(1 - lax.axis_index("core"), t_ref, held, sems)
    for copy in copies:
        copy.start()
    for j in range(blocks):
        copies[j].wait()
        out_ref[:, j * size : (j + 1) * size, :] = jnp.swapaxes(held[j], 0, 1)


def join_kernel(t_ref, got_ref, out_ref, held, sems, got_sem):
    blocks, size = held.shape[:2]
    cols = held.shape[3]
    copies = fetches(lax.axis_index("core"), t_ref, held, sems)
    for copy in copies:
        copy.start()
    right = pltpu.make_async_copy(got_ref, out_ref.at[:, :, cols:], got_sem)
    right.start()
    for j in range(blocks):
        copies[j].wait()
        out_ref[:, j * size : (j + 1) * size, :cols] = jnp.swapaxes(held[j], 0, 1)
    right.wait()


def give(t):
    blocks, _, size, phys, cols = t.shape
    return pl.pallas_call(
        give_kernel,
        out_shape=jax.ShapeDtypeStruct((phys, blocks * size, cols), t.dtype),
        in_specs=[HBM],
        out_specs=VMEM,
        scratch_shapes=[
            pltpu.VMEM((blocks, size, phys, cols), t.dtype),
            pltpu.SemaphoreType.DMA((blocks,)),
        ],
        compiler_params=pltpu.CompilerParams(vmem_limit_bytes=56 * 2**20),
    )(t)


def join(t, got):
    blocks, _, size, phys, cols = t.shape
    return pl.pallas_call(
        join_kernel,
        out_shape=pltpu.VMEM((phys, blocks * size, 2 * cols), t.dtype),
        in_specs=[HBM, VMEM],
        out_specs=VMEM,
        scratch_shapes=[
            pltpu.VMEM((blocks, size, phys, cols), t.dtype),
            pltpu.SemaphoreType.DMA((blocks,)),
            pltpu.SemaphoreType.DMA,
        ],
        compiler_params=pltpu.CompilerParams(vmem_limit_bytes=40 * 2**20),
    )(t, got)


def contract_kernel(*refs):
    *x_refs, w_ref, own_ref, part_ref, mixed_in_ref, other_in_ref, mixed_ref, other_ref = refs
    add(x_refs, w_ref, own_ref, part_ref, mixed_in_ref[...], other_in_ref[...], mixed_ref, other_ref, True)


def open_kernel(*refs):
    *x_refs, w_ref, own_ref, part_ref, mixed_ref, other_ref = refs
    zeros = [jnp.zeros(ref.shape, jnp.float32) for ref in (mixed_ref, other_ref)]
    add(x_refs, w_ref, own_ref, part_ref, *zeros, mixed_ref, other_ref, False)


def add(x_refs, w_ref, own_ref, part_ref, mixed, other, mixed_ref, other_ref, last):
    cols = mixed_ref.shape[1]
    blocks = [ref[j] for ref in x_refs for j in range(NY)]
    rows = jnp.concatenate(blocks, axis=1)
    depth = rows.shape[1]
    bonds = pl.ds(w_ref.shape[1] - depth if last else 0, depth)
    other, squares = other[:, :cols], other[:, cols:]
    total = None
    for block in blocks:
        wide = block.astype(jnp.float32)
        total = wide * wide if total is None else total + wide * wide
    for p in range(w_ref.shape[0]):
        prod = jnp.dot(rows, w_ref[p, bonds, :], preferred_element_type=jnp.float32)
        mixed += own_ref[:, p : p + 1] * prod[:, :cols]
        other += part_ref[:, p : p + 1] * prod[:, cols:]
    squares = squares + jnp.broadcast_to(jnp.sum(total, axis=1, keepdims=True), squares.shape)
    mixed_ref[...] = mixed
    other_ref[:, :cols] = other
    other_ref[:, cols:] = squares


def part_of(kernel, *operands):
    rows, cols = operands[0].shape[1:]
    return pl.pallas_call(
        kernel,
        out_shape=(
            jax.ShapeDtypeStruct((rows, cols), jnp.float32),
            jax.ShapeDtypeStruct((rows, 2 * cols), jnp.float32),
        ),
        in_specs=[VMEM] * len(operands),
        out_specs=(VMEM, VMEM),
        compiler_params=pltpu.CompilerParams(vmem_limit_bytes=16 * 2**20),
    )(*operands)


def contract(near, far, w, own, part):
    begun = part_of(open_kernel, near, far[0], w, own, part)
    return part_of(contract_kernel, *far[1:], w, own, part, *begun)


def local(start_rows, site_tensors, block_scales, displacement, outcomes):
    sites = lax.axis_size("site")
    chi, phys, cols = site_tensors.shape[1:]
    allrows = start_rows.shape[0]
    ngroups = -(-allrows // ROWS)
    bodies = ngroups + sites - 1
    position = lax.axis_index("site")
    devices = list(itertools.product(range(sites), range(NZ), range(NY), range(NC)))

    def index(site, z, y, core):
        return ((site % sites * NZ + z % NZ) * NY + y % NY) * NC + core

    def shifted(value, hop, first, second):
        pairs = []
        for site, z, y, core in devices:
            up, right = (second, first) if core == 0 else (first, second)
            pairs.append((index(site, z, y, core), index(site + hop, z + up, y + right, core)))
        return lax.ppermute(value, ("site",) + BOND, pairs)

    def to_partner(value):
        return lax.ppermute(value, "core", [(0, 1), (1, 0)])

    def ahead(value):
        return [shifted(value, 1, shift, 0) for shift in FIRST]

    def along_second(value):
        return [shifted(value, 0, 0, shift) for shift in SECOND]

    def start_piece(batch):
        first = min(batch, ngroups - 1) * STRIDE
        return start_rows[first : first + ROWS]

    tensor = site_tensors[0].reshape(NZ * NY, NC, cols, phys, cols)
    scale = block_scales[0][:, 0]
    partner_scale = to_partner(scale)
    onehot = (outcomes[0][:, None] == jnp.arange(phys, dtype=jnp.int32)[None, :]).astype(jnp.float32)
    weight = jnp.dot(onehot, displacement[0], precision=lax.Precision.HIGHEST)
    own_coef = weight * scale[None, :]
    part_coef = weight * partner_scale[None, :]
    def coefficients(body):
        first = jnp.clip(body - position, 0, ngroups - 1) * STRIDE
        return [lax.dynamic_slice_in_dim(c, first, ROWS, 0) for c in (own_coef, part_coef)]

    coefs = [coefficients(body) for body in range(bodies)]
    arriving = {0: ahead(start_piece(0))}
    sent = give(tensor)
    sent, coefs, closing, at_site = lax.optimization_barrier(
        (sent, coefs, position == sites - 1, [position == s for s in range(sites - 1)])
    )
    got = to_partner(sent)
    near = jnp.stack(arriving.pop(0))
    far = along_second(near)
    w = join(tensor, got)
    leaves, norms = [], []
    for body in range(bodies):
        more = body + 1 < bodies
        mixed, other = contract(near, far, w, *coefs[body])
        arrived = to_partner(other)
        norm = jnp.sqrt((other[:, cols:] + arrived[:, cols:]) / chi + 1e-06)
        leave = ((mixed + arrived[:, :cols]) / norm).astype(jnp.bfloat16)
        leaves.append(leave)
        norms.append(norm[:, 0])
        if more:
            arriving[body + 1] = ahead(jnp.where(closing, start_piece(body + 1), leave))
        if more:
            near = jnp.stack(arriving.pop(body + 1))
            far = along_second(near)
    leaves, norms = lax.optimization_barrier((leaves, norms))

    def placed(pieces):
        rows = []
        for b in range(ngroups):
            piece = pieces[b + sites - 1]
            for s in range(sites - 1):
                piece = jnp.where(at_site[s], pieces[b + s], piece)
            rows.append(piece if b + 1 == ngroups else piece[:STRIDE])
        return jnp.concatenate(rows, 0)

    return (placed(leaves)[None], jnp.log(placed(norms))[None])


def solution(mesh):
    fine = Mesh(mesh.devices.reshape(-1, NZ, NY, NC), ("site",) + BOND)
    return jax.shard_map(
        local,
        mesh=fine,
        in_specs=(
            P(None, BOND),
            P("site", None, None, BOND),
            P("site", None, BOND),
            P("site", None, None),
            P("site", None),
        ),
        out_specs=(P("site", None, BOND), P("site", None)),
        check_vma=False,
    )
```

```python
import itertools

import jax
import jax.numpy as jnp
from jax import lax
from jax.experimental import pallas as pl
from jax.experimental.pallas import tpu as pltpu
from jax.sharding import Mesh, PartitionSpec as P

ROWS = 256
STRIDE = 256
NZ, NY, NC = 4, 4, 2
FIRST = (0, 1, 2, 3)
SECOND = (2, 1, 3)
BOND = ("z", "y", "core")
VMEM = pl.BlockSpec(memory_space=pltpu.VMEM)
HBM = pl.BlockSpec(memory_space=pltpu.HBM)


def fetch(parity, t_ref, held, sems):
    z, y = lax.axis_index("z"), lax.axis_index("y")
    for i, second in enumerate((0,) + SECOND):
        for k, first in enumerate(FIRST):
            back_z = (1 - parity) * second + parity * first
            back_y = (1 - parity) * first + parity * second
            block = lax.rem(z - back_z + NZ, NZ) * NY + lax.rem(y - back_y + NY, NY)
            j = i * NY + k
            pltpu.make_async_copy(t_ref.at[block, parity], held.at[j], sems.at[j]).start()


def turn(t_ref, out_ref, held, sems):
    blocks, size, _, cols = held.shape

    def step(j, carry):
        pltpu.make_async_copy(t_ref.at[0, 0], held.at[j], sems.at[j]).wait()
        bonds = pl.ds(pl.multiple_of(j * size, size), size)
        out_ref[:, bonds, pl.ds(0, cols)] = jnp.swapaxes(held[j], 0, 1)
        return carry

    lax.fori_loop(0, blocks, step, 0)


def give_kernel(t_ref, out_ref, held, sems):
    fetch(1 - lax.axis_index("core"), t_ref, held, sems)
    turn(t_ref, out_ref, held, sems)


def join_kernel(t_ref, got_ref, out_ref, held, sems, got_sem):
    cols = held.shape[3]
    fetch(lax.axis_index("core"), t_ref, held, sems)
    right = pltpu.make_async_copy(got_ref, out_ref.at[:, :, cols:], got_sem)
    right.start()
    turn(t_ref, out_ref, held, sems)
    right.wait()


def give(t):
    blocks, _, size, phys, cols = t.shape
    return pl.pallas_call(
        give_kernel,
        out_shape=jax.ShapeDtypeStruct((phys, blocks * size, cols), t.dtype),
        in_specs=[HBM],
        out_specs=VMEM,
        scratch_shapes=[
            pltpu.VMEM((blocks, size, phys, cols), t.dtype),
            pltpu.SemaphoreType.DMA((blocks,)),
        ],
        compiler_params=pltpu.CompilerParams(vmem_limit_bytes=56 * 2**20),
    )(t)


def join(t, got):
    blocks, _, size, phys, cols = t.shape
    return pl.pallas_call(
        join_kernel,
        out_shape=pltpu.VMEM((phys, blocks * size, 2 * cols), t.dtype),
        in_specs=[HBM, VMEM],
        out_specs=VMEM,
        scratch_shapes=[
            pltpu.VMEM((blocks, size, phys, cols), t.dtype),
            pltpu.SemaphoreType.DMA((blocks,)),
            pltpu.SemaphoreType.DMA,
        ],
        compiler_params=pltpu.CompilerParams(vmem_limit_bytes=40 * 2**20),
    )(t, got)


def contract_kernel(*refs):
    *x_refs, w_ref, own_ref, part_ref, mixed_in_ref, other_in_ref, mixed_ref, other_ref = refs
    add(x_refs, w_ref, own_ref, part_ref, mixed_in_ref[...], other_in_ref[...], mixed_ref, other_ref, True)


def open_kernel(*refs):
    *x_refs, w_ref, own_ref, part_ref, mixed_ref, other_ref = refs
    zeros = [jnp.zeros(ref.shape, jnp.float32) for ref in (mixed_ref, other_ref)]
    add(x_refs, w_ref, own_ref, part_ref, *zeros, mixed_ref, other_ref, False)


def add(x_refs, w_ref, own_ref, part_ref, mixed, other, mixed_ref, other_ref, last):
    cols = mixed_ref.shape[1]
    blocks = [ref[j] for ref in x_refs for j in range(NY)]
    rows = jnp.concatenate(blocks, axis=1)
    depth = rows.shape[1]
    bonds = pl.ds(w_ref.shape[1] - depth if last else 0, depth)
    other, squares = other[:, :cols], other[:, cols:]
    total = None
    for block in blocks:
        wide = block.astype(jnp.float32)
        total = wide * wide if total is None else total + wide * wide
    squares = squares + jnp.broadcast_to(jnp.sum(total, axis=1, keepdims=True), squares.shape)
    mixed_ref[...] = mixed
    other_ref[:, :cols] = other
    other_ref[:, cols:] = squares
    lane = lax.broadcasted_iota(jnp.int32, own_ref.shape, 1)

    def step(p, carry):
        prod = jnp.dot(rows, w_ref[p, bonds, :], preferred_element_type=jnp.float32)
        own, part = (
            jnp.sum(jnp.where(lane == p, ref[...], 0.0), axis=1, keepdims=True)
            for ref in (own_ref, part_ref)
        )
        mixed_ref[...] += own * prod[:, :cols]
        other_ref[:, :cols] += part * prod[:, cols:]
        return carry

    lax.fori_loop(0, w_ref.shape[0], step, 0, unroll=4)


def part_of(kernel, *operands):
    rows, cols = operands[0].shape[1:]
    return pl.pallas_call(
        kernel,
        out_shape=(
            jax.ShapeDtypeStruct((rows, cols), jnp.float32),
            jax.ShapeDtypeStruct((rows, 2 * cols), jnp.float32),
        ),
        in_specs=[VMEM] * len(operands),
        out_specs=(VMEM, VMEM),
        compiler_params=pltpu.CompilerParams(vmem_limit_bytes=16 * 2**20),
    )(*operands)


def contract(near, far, w, own, part):
    begun = part_of(open_kernel, near, far[0], w, own, part)
    return part_of(contract_kernel, *far[1:], w, own, part, *begun)


def local(start_rows, site_tensors, block_scales, displacement, outcomes):
    sites = lax.axis_size("site")
    chi, phys, cols = site_tensors.shape[1:]
    allrows = start_rows.shape[0]
    ngroups = -(-allrows // ROWS)
    bodies = ngroups + sites - 1
    position = lax.axis_index("site")
    devices = list(itertools.product(range(sites), range(NZ), range(NY), range(NC)))

    def index(site, z, y, core):
        return ((site % sites * NZ + z % NZ) * NY + y % NY) * NC + core

    def shifted(value, hop, first, second):
        pairs = []
        for site, z, y, core in devices:
            up, right = (second, first) if core == 0 else (first, second)
            pairs.append((index(site, z, y, core), index(site + hop, z + up, y + right, core)))
        return lax.ppermute(value, ("site",) + BOND, pairs)

    def to_partner(value):
        return lax.ppermute(value, "core", [(0, 1), (1, 0)])

    def ahead(value):
        return [shifted(value, 1, shift, 0) for shift in FIRST]

    def along_second(value):
        return [shifted(value, 0, 0, shift) for shift in SECOND]

    def start_piece(batch):
        first = min(batch, ngroups - 1) * STRIDE
        return start_rows[first : first + ROWS]

    tensor = site_tensors[0].reshape(NZ * NY, NC, cols, phys, cols)
    scale = block_scales[0][:, 0]
    partner_scale = to_partner(scale)
    onehot = (outcomes[0][:, None] == jnp.arange(phys, dtype=jnp.int32)[None, :]).astype(jnp.float32)
    weight = jnp.dot(onehot, displacement[0], precision=lax.Precision.HIGHEST)
    own_coef = weight * scale[None, :]
    part_coef = weight * partner_scale[None, :]
    def coefficients(body):
        first = jnp.clip(body - position, 0, ngroups - 1) * STRIDE
        return [lax.dynamic_slice_in_dim(c, first, ROWS, 0) for c in (own_coef, part_coef)]

    coefs = [coefficients(body) for body in range(bodies)]
    arriving = {0: ahead(start_piece(0))}
    sent = give(tensor)
    sent, coefs, closing, at_site = lax.optimization_barrier(
        (sent, coefs, position == sites - 1, [position == s for s in range(sites - 1)])
    )
    got = to_partner(sent)
    near = jnp.stack(arriving.pop(0))
    far = along_second(near)
    w = join(tensor, got)
    leaves, norms = [], []
    for body in range(bodies):
        more = body + 1 < bodies
        mixed, other = contract(near, far, w, *coefs[body])
        arrived = to_partner(other)
        norm = jnp.sqrt((other[:, cols:] + arrived[:, cols:]) / chi + 1e-06)
        leave = ((mixed + arrived[:, :cols]) / norm).astype(jnp.bfloat16)
        leaves.append(leave)
        norms.append(norm[:, 0])
        if more:
            arriving[body + 1] = ahead(jnp.where(closing, start_piece(body + 1), leave))
        if more:
            near = jnp.stack(arriving.pop(body + 1))
            far = along_second(near)
    leaves, norms = lax.optimization_barrier((leaves, norms))

    def placed(pieces):
        rows = []
        for b in range(ngroups):
            piece = pieces[b + sites - 1]
            for s in range(sites - 1):
                piece = jnp.where(at_site[s], pieces[b + s], piece)
            rows.append(piece if b + 1 == ngroups else piece[:STRIDE])
        return jnp.concatenate(rows, 0)

    return (placed(leaves)[None], jnp.log(placed(norms))[None])


def solution(mesh):
    fine = Mesh(mesh.devices.reshape(-1, NZ, NY, NC), ("site",) + BOND)
    return jax.shard_map(
        local,
        mesh=fine,
        in_specs=(
            P(None, BOND),
            P("site", None, None, BOND),
            P("site", None, BOND),
            P("site", None, None),
            P("site", None),
        ),
        out_specs=(P("site", None, BOND), P("site", None)),
        check_vma=False,
    )
```

```python
import itertools

import jax
import jax.numpy as jnp
from jax import lax
from jax.experimental import pallas as pl
from jax.experimental.pallas import tpu as pltpu
from jax.sharding import Mesh, PartitionSpec as P

ROWS = 256
STRIDE = 256
NZ, NY, NC = 4, 4, 2
FIRST = (0, 1, 2, 3)
SECOND = (2, 1, 3)
BOND = ("z", "y", "core")
VMEM = pl.BlockSpec(memory_space=pltpu.VMEM)
HBM = pl.BlockSpec(memory_space=pltpu.HBM)


def fetch(parity, t_ref, held, sems):
    z, y = lax.axis_index("z"), lax.axis_index("y")
    for i, second in enumerate((0,) + SECOND):
        for k, first in enumerate(FIRST):
            back_z = (1 - parity) * second + parity * first
            back_y = (1 - parity) * first + parity * second
            block = lax.rem(z - back_z + NZ, NZ) * NY + lax.rem(y - back_y + NY, NY)
            j = i * NY + k
            pltpu.make_async_copy(t_ref.at[block, parity], held.at[j], sems.at[j]).start()


def turn(t_ref, out_ref, held, sems, then=lambda j: None):
    blocks, size, _, cols = held.shape

    def step(j, carry):
        pltpu.make_async_copy(t_ref.at[0, 0], held.at[j], sems.at[j]).wait()
        bonds = pl.ds(pl.multiple_of(j * size, size), size)
        out_ref[:, bonds, pl.ds(0, cols)] = jnp.swapaxes(held[j], 0, 1)
        then(j)
        return carry

    lax.fori_loop(0, blocks, step, 0)


def give_kernel(t_ref, out_ref, held, turned, sems, out_sems):
    blocks, size = held.shape[:2]
    fetch(1 - lax.axis_index("core"), t_ref, held, sems)

    def store(j):
        bonds = pl.ds(pl.multiple_of(j * size, size), size)
        return pltpu.make_async_copy(turned.at[:, bonds, :], out_ref.at[:, bonds, :], out_sems.at[j])

    turn(t_ref, turned, held, sems, lambda j: store(j).start())

    def step(j, carry):
        store(j).wait()
        return carry

    lax.fori_loop(0, blocks, step, 0)


def join_kernel(t_ref, got_ref, out_ref, held, sems, got_sem):
    cols = held.shape[3]
    fetch(lax.axis_index("core"), t_ref, held, sems)
    right = pltpu.make_async_copy(got_ref, out_ref.at[:, :, cols:], got_sem)
    right.start()
    turn(t_ref, out_ref, held, sems)
    right.wait()


def give(t):
    blocks, _, size, phys, cols = t.shape
    return pl.pallas_call(
        give_kernel,
        out_shape=jax.ShapeDtypeStruct((phys, blocks * size, cols), t.dtype),
        in_specs=[HBM],
        out_specs=HBM,
        scratch_shapes=[
            pltpu.VMEM((blocks, size, phys, cols), t.dtype),
            pltpu.VMEM((phys, blocks * size, cols), t.dtype),
            pltpu.SemaphoreType.DMA((blocks,)),
            pltpu.SemaphoreType.DMA((blocks,)),
        ],
        compiler_params=pltpu.CompilerParams(vmem_limit_bytes=56 * 2**20),
    )(t)


def join(t, got):
    blocks, _, size, phys, cols = t.shape
    return pl.pallas_call(
        join_kernel,
        out_shape=pltpu.VMEM((phys, blocks * size, 2 * cols), t.dtype),
        in_specs=[HBM, VMEM],
        out_specs=VMEM,
        scratch_shapes=[
            pltpu.VMEM((blocks, size, phys, cols), t.dtype),
            pltpu.SemaphoreType.DMA((blocks,)),
            pltpu.SemaphoreType.DMA,
        ],
        compiler_params=pltpu.CompilerParams(vmem_limit_bytes=40 * 2**20),
    )(t, got)


def contract_kernel(*refs):
    *x_refs, w_ref, own_ref, part_ref, mixed_in_ref, other_in_ref, mixed_ref, other_ref = refs
    add(x_refs, w_ref, own_ref, part_ref, mixed_in_ref[...], other_in_ref[...], mixed_ref, other_ref, True, 8)


def open_kernel(*refs):
    *x_refs, w_ref, own_ref, part_ref, mixed_ref, other_ref = refs
    zeros = [jnp.zeros(ref.shape, jnp.float32) for ref in (mixed_ref, other_ref)]
    add(x_refs, w_ref, own_ref, part_ref, *zeros, mixed_ref, other_ref, False, 1)


def add(x_refs, w_ref, own_ref, part_ref, mixed, other, mixed_ref, other_ref, last, unroll):
    cols = mixed_ref.shape[1]
    blocks = [ref[j] for ref in x_refs for j in range(NY)]
    rows = jnp.concatenate(blocks, axis=1)
    depth = rows.shape[1]
    bonds = pl.ds(w_ref.shape[1] - depth if last else 0, depth)
    other, squares = other[:, :cols], other[:, cols:]
    total = None
    for block in blocks:
        wide = block.astype(jnp.float32)
        total = wide * wide if total is None else total + wide * wide
    squares = squares + jnp.broadcast_to(jnp.sum(total, axis=1, keepdims=True), squares.shape)
    mixed_ref[...] = mixed
    other_ref[:, :cols] = other
    other_ref[:, cols:] = squares
    lane = lax.broadcasted_iota(jnp.int32, own_ref.shape, 1)

    def step(p, carry):
        prod = jnp.dot(rows, w_ref[p, bonds, :], preferred_element_type=jnp.float32)
        own, part = (
            jnp.sum(jnp.where(lane == p, ref[...], 0.0), axis=1, keepdims=True)
            for ref in (own_ref, part_ref)
        )
        mixed_ref[...] += own * prod[:, :cols]
        other_ref[:, :cols] += part * prod[:, cols:]
        return carry

    lax.fori_loop(0, w_ref.shape[0], step, 0, unroll=unroll)


def part_of(kernel, *operands):
    rows, cols = operands[0].shape[1:]
    return pl.pallas_call(
        kernel,
        out_shape=(
            jax.ShapeDtypeStruct((rows, cols), jnp.float32),
            jax.ShapeDtypeStruct((rows, 2 * cols), jnp.float32),
        ),
        in_specs=[VMEM] * len(operands),
        out_specs=(VMEM, VMEM),
        compiler_params=pltpu.CompilerParams(vmem_limit_bytes=16 * 2**20),
    )(*operands)


def contract(near, far, w, own, part):
    begun = part_of(open_kernel, near, far[0], w, own, part)
    return part_of(contract_kernel, *far[1:], w, own, part, *begun)


def local(start_rows, site_tensors, block_scales, displacement, outcomes):
    sites = lax.axis_size("site")
    chi, phys, cols = site_tensors.shape[1:]
    allrows = start_rows.shape[0]
    ngroups = -(-allrows // ROWS)
    bodies = ngroups + sites - 1
    position = lax.axis_index("site")
    devices = list(itertools.product(range(sites), range(NZ), range(NY), range(NC)))

    def index(site, z, y, core):
        return ((site % sites * NZ + z % NZ) * NY + y % NY) * NC + core

    def shifted(value, hop, first, second):
        pairs = []
        for site, z, y, core in devices:
            up, right = (second, first) if core == 0 else (first, second)
            pairs.append((index(site, z, y, core), index(site + hop, z + up, y + right, core)))
        return lax.ppermute(value, ("site",) + BOND, pairs)

    def to_partner(value):
        return lax.ppermute(value, "core", [(0, 1), (1, 0)])

    def ahead(value):
        return [shifted(value, 1, shift, 0) for shift in FIRST]

    def along_second(value):
        return [shifted(value, 0, 0, shift) for shift in SECOND]

    def start_piece(batch):
        first = min(batch, ngroups - 1) * STRIDE
        return start_rows[first : first + ROWS]

    tensor = site_tensors[0].reshape(NZ * NY, NC, cols, phys, cols)
    scale = block_scales[0][:, 0]
    partner_scale = to_partner(scale)
    onehot = (outcomes[0][:, None] == jnp.arange(phys, dtype=jnp.int32)[None, :]).astype(jnp.float32)
    weight = jnp.dot(onehot, displacement[0], precision=lax.Precision.HIGHEST)
    own_coef = weight * scale[None, :]
    part_coef = weight * partner_scale[None, :]
    def coefficients(body):
        first = jnp.clip(body - position, 0, ngroups - 1) * STRIDE
        return [lax.dynamic_slice_in_dim(c, first, ROWS, 0) for c in (own_coef, part_coef)]

    coefs = [coefficients(body) for body in range(bodies)]
    arriving = {0: ahead(start_piece(0))}
    sent = give(tensor)
    sent, coefs, closing, at_site = lax.optimization_barrier(
        (sent, coefs, position == sites - 1, [position == s for s in range(sites - 1)])
    )
    got = to_partner(sent)
    near = jnp.stack(arriving.pop(0))
    far = along_second(near)
    w = join(tensor, got)
    leaves, norms = [], []
    for body in range(bodies):
        more = body + 1 < bodies
        mixed, other = contract(near, far, w, *coefs[body])
        arrived = to_partner(other)
        norm = jnp.sqrt((other[:, cols:] + arrived[:, cols:]) / chi + 1e-06)
        leave = ((mixed + arrived[:, :cols]) / norm).astype(jnp.bfloat16)
        leaves.append(leave)
        norms.append(norm[:, 0])
        if more:
            arriving[body + 1] = ahead(jnp.where(closing, start_piece(body + 1), leave))
        if more:
            near = jnp.stack(arriving.pop(body + 1))
            far = along_second(near)
    leaves, norms = lax.optimization_barrier((leaves, norms))

    def placed(pieces):
        rows = []
        for b in range(ngroups):
            piece = pieces[b + sites - 1]
            for s in range(sites - 1):
                piece = jnp.where(at_site[s], pieces[b + s], piece)
            rows.append(piece if b + 1 == ngroups else piece[:STRIDE])
        return jnp.concatenate(rows, 0)

    return (placed(leaves)[None], jnp.log(placed(norms))[None])


def solution(mesh):
    fine = Mesh(mesh.devices.reshape(-1, NZ, NY, NC), ("site",) + BOND)
    return jax.shard_map(
        local,
        mesh=fine,
        in_specs=(
            P(None, BOND),
            P("site", None, None, BOND),
            P("site", None, BOND),
            P("site", None, None),
            P("site", None),
        ),
        out_specs=(P("site", None, BOND), P("site", None)),
        check_vma=False,
    )
```

```python
import itertools

import jax
import jax.numpy as jnp
from jax import lax
from jax.experimental import pallas as pl
from jax.experimental.pallas import tpu as pltpu
from jax.sharding import Mesh, PartitionSpec as P

ROWS = 352
STRIDE = 336
NZ, NY, NC = 4, 4, 2
FIRST = (0, 1, 2, 3)
SECOND = (2, 1, 3)
BOND = ("z", "y", "core")
VMEM = pl.BlockSpec(memory_space=pltpu.VMEM)
HBM = pl.BlockSpec(memory_space=pltpu.HBM)


def fetch(parity, t_ref, held, sems):
    z, y = lax.axis_index("z"), lax.axis_index("y")
    for i, second in enumerate((0,) + SECOND):
        for k, first in enumerate(FIRST):
            back_z = (1 - parity) * second + parity * first
            back_y = (1 - parity) * first + parity * second
            block = lax.rem(z - back_z + NZ, NZ) * NY + lax.rem(y - back_y + NY, NY)
            j = i * NY + k
            pltpu.make_async_copy(t_ref.at[block, parity], held.at[j], sems.at[j]).start()


def turn(t_ref, out_ref, held, sems, then=lambda j: None):
    blocks, size, _, cols = held.shape

    def step(j, carry):
        pltpu.make_async_copy(t_ref.at[0, 0], held.at[j], sems.at[j]).wait()
        bonds = pl.ds(pl.multiple_of(j * size, size), size)
        out_ref[:, bonds, pl.ds(0, cols)] = jnp.swapaxes(held[j], 0, 1)
        then(j)
        return carry

    lax.fori_loop(0, blocks, step, 0)


def give_kernel(t_ref, out_ref, held, turned, sems, out_sems):
    blocks, size = held.shape[:2]
    fetch(1 - lax.axis_index("core"), t_ref, held, sems)

    def store(j):
        bonds = pl.ds(pl.multiple_of(j * size, size), size)
        return pltpu.make_async_copy(turned.at[:, bonds, :], out_ref.at[:, bonds, :], out_sems.at[j])

    turn(t_ref, turned, held, sems, lambda j: store(j).start())

    def step(j, carry):
        store(j).wait()
        return carry

    lax.fori_loop(0, blocks, step, 0)


def join_kernel(t_ref, got_ref, out_ref, held, sems, got_sem):
    cols = held.shape[3]
    fetch(lax.axis_index("core"), t_ref, held, sems)
    right = pltpu.make_async_copy(got_ref, out_ref.at[:, :, cols:], got_sem)
    right.start()
    turn(t_ref, out_ref, held, sems)
    right.wait()


def give(t):
    blocks, _, size, phys, cols = t.shape
    return pl.pallas_call(
        give_kernel,
        out_shape=jax.ShapeDtypeStruct((phys, blocks * size, cols), t.dtype),
        in_specs=[HBM],
        out_specs=HBM,
        scratch_shapes=[
            pltpu.VMEM((blocks, size, phys, cols), t.dtype),
            pltpu.VMEM((phys, blocks * size, cols), t.dtype),
            pltpu.SemaphoreType.DMA((blocks,)),
            pltpu.SemaphoreType.DMA((blocks,)),
        ],
        compiler_params=pltpu.CompilerParams(vmem_limit_bytes=56 * 2**20),
    )(t)


def join(t, got):
    blocks, _, size, phys, cols = t.shape
    return pl.pallas_call(
        join_kernel,
        out_shape=pltpu.VMEM((phys, blocks * size, 2 * cols), t.dtype),
        in_specs=[HBM, VMEM],
        out_specs=VMEM,
        scratch_shapes=[
            pltpu.VMEM((blocks, size, phys, cols), t.dtype),
            pltpu.SemaphoreType.DMA((blocks,)),
            pltpu.SemaphoreType.DMA,
        ],
        compiler_params=pltpu.CompilerParams(vmem_limit_bytes=40 * 2**20),
    )(t, got)


def contract_kernel(*refs):
    *x_refs, w_ref, own_ref, part_ref, mixed_in_ref, other_in_ref, mixed_ref, other_ref = refs
    add(x_refs, w_ref, own_ref, part_ref, mixed_in_ref[...], other_in_ref[...], mixed_ref, other_ref, True, 8)


def open_kernel(*refs):
    *x_refs, w_ref, own_ref, part_ref, mixed_ref, other_ref = refs
    zeros = [jnp.zeros(ref.shape, jnp.float32) for ref in (mixed_ref, other_ref)]
    add(x_refs, w_ref, own_ref, part_ref, *zeros, mixed_ref, other_ref, False, 1)


def add(x_refs, w_ref, own_ref, part_ref, mixed, other, mixed_ref, other_ref, last, unroll):
    cols = mixed_ref.shape[1]
    blocks = [ref[j] for ref in x_refs for j in range(NY)]
    rows = jnp.concatenate(blocks, axis=1)
    depth = rows.shape[1]
    bonds = pl.ds(w_ref.shape[1] - depth if last else 0, depth)
    other, squares = other[:, :cols], other[:, cols:]
    total = None
    for block in blocks:
        wide = block.astype(jnp.float32)
        total = wide * wide if total is None else total + wide * wide
    squares = squares + jnp.broadcast_to(jnp.sum(total, axis=1, keepdims=True), squares.shape)
    mixed_ref[...] = mixed
    other_ref[:, :cols] = other
    other_ref[:, cols:] = squares
    lane = lax.broadcasted_iota(jnp.int32, own_ref.shape, 1)

    def step(p, carry):
        prod = jnp.dot(rows, w_ref[p, bonds, :], preferred_element_type=jnp.float32)
        own, part = (
            jnp.sum(jnp.where(lane == p, ref[...], 0.0), axis=1, keepdims=True)
            for ref in (own_ref, part_ref)
        )
        mixed_ref[...] += own * prod[:, :cols]
        other_ref[:, :cols] += part * prod[:, cols:]
        return carry

    lax.fori_loop(0, w_ref.shape[0], step, 0, unroll=unroll)


def part_of(kernel, *operands):
    rows, cols = operands[0].shape[1:]
    return pl.pallas_call(
        kernel,
        out_shape=(
            jax.ShapeDtypeStruct((rows, cols), jnp.float32),
            jax.ShapeDtypeStruct((rows, 2 * cols), jnp.float32),
        ),
        in_specs=[VMEM] * len(operands),
        out_specs=(VMEM, VMEM),
        compiler_params=pltpu.CompilerParams(vmem_limit_bytes=20 * 2**20),
    )(*operands)


def contract(near, far, w, own, part):
    begun = part_of(open_kernel, near, far[0], w, own, part)
    return part_of(contract_kernel, *far[1:], w, own, part, *begun)


def local(start_rows, site_tensors, block_scales, displacement, outcomes):
    sites = lax.axis_size("site")
    chi, phys, cols = site_tensors.shape[1:]
    allrows = start_rows.shape[0]
    ngroups = -(-allrows // ROWS)
    bodies = ngroups + sites - 1
    position = lax.axis_index("site")
    devices = list(itertools.product(range(sites), range(NZ), range(NY), range(NC)))

    def index(site, z, y, core):
        return ((site % sites * NZ + z % NZ) * NY + y % NY) * NC + core

    def shifted(value, hop, first, second):
        pairs = []
        for site, z, y, core in devices:
            up, right = (second, first) if core == 0 else (first, second)
            pairs.append((index(site, z, y, core), index(site + hop, z + up, y + right, core)))
        return lax.ppermute(value, ("site",) + BOND, pairs)

    def to_partner(value):
        return lax.ppermute(value, "core", [(0, 1), (1, 0)])

    def ahead(value):
        return [shifted(value, 1, shift, 0) for shift in FIRST]

    def along_second(value):
        return [shifted(value, 0, 0, shift) for shift in SECOND]

    def start_piece(batch):
        first = min(batch, ngroups - 1) * STRIDE
        return start_rows[first : first + ROWS]

    tensor = site_tensors[0].reshape(NZ * NY, NC, cols, phys, cols)
    scale = block_scales[0][:, 0]
    partner_scale = to_partner(scale)
    onehot = (outcomes[0][:, None] == jnp.arange(phys, dtype=jnp.int32)[None, :]).astype(jnp.float32)
    weight = jnp.dot(onehot, displacement[0], precision=lax.Precision.HIGHEST)
    own_coef = weight * scale[None, :]
    part_coef = weight * partner_scale[None, :]
    def coefficients(body):
        first = jnp.clip(body - position, 0, ngroups - 1) * STRIDE
        return [lax.dynamic_slice_in_dim(c, first, ROWS, 0) for c in (own_coef, part_coef)]

    coefs = [coefficients(body) for body in range(bodies)]
    arriving = {0: ahead(start_piece(0))}
    sent = give(tensor)
    sent, coefs, closing, at_site = lax.optimization_barrier(
        (sent, coefs, position == sites - 1, [position == s for s in range(sites - 1)])
    )
    got = to_partner(sent)
    near = jnp.stack(arriving.pop(0))
    far = along_second(near)
    w = join(tensor, got)
    leaves, norms = [], []
    for body in range(bodies):
        more = body + 1 < bodies
        mixed, other = contract(near, far, w, *coefs[body])
        arrived = to_partner(other)
        norm = jnp.sqrt((other[:, cols:] + arrived[:, cols:]) / chi + 1e-06)
        leave = ((mixed + arrived[:, :cols]) / norm).astype(jnp.bfloat16)
        leaves.append(leave)
        norms.append(norm[:, 0])
        if more:
            arriving[body + 1] = ahead(jnp.where(closing, start_piece(body + 1), leave))
        if more:
            near = jnp.stack(arriving.pop(body + 1))
            far = along_second(near)
    leaves, norms = lax.optimization_barrier((leaves, norms))

    def placed(pieces):
        rows = []
        for b in range(ngroups):
            piece = pieces[b + sites - 1]
            for s in range(sites - 1):
                piece = jnp.where(at_site[s], pieces[b + s], piece)
            rows.append(piece if b + 1 == ngroups else piece[:STRIDE])
        return jnp.concatenate(rows, 0)

    return (placed(leaves)[None], jnp.log(placed(norms))[None])


def solution(mesh):
    fine = Mesh(mesh.devices.reshape(-1, NZ, NY, NC), ("site",) + BOND)
    return jax.shard_map(
        local,
        mesh=fine,
        in_specs=(
            P(None, BOND),
            P("site", None, None, BOND),
            P("site", None, BOND),
            P("site", None, None),
            P("site", None),
        ),
        out_specs=(P("site", None, BOND), P("site", None)),
        check_vma=False,
    )
```
